256 devices in a mesh: row: 32 (over y, x, z_lo), col: 8 (over z_hi, core).
Axes of the slice: x: 4, y: 4, z: 8 (z_hi: 4, z_lo: 2; z = z_hi * 2 + z_lo), core: 2. Of those that a mesh axis runs over, the one named last changes fastest.
Arguments:
- matrix_tiles: float32 [32, 8, 32, 256, 256], P('row', 'col'), may hold values from -0.25 to 0.25
- tile_rows: int32 [32, 8, 32], P('row', 'col'), may hold values from 0 to 63, as said below
- tile_cols: int32 [32, 8, 32], P('row', 'col'), may hold values from 0 to 255, as said below
- tile_count: int32 [32, 8], P('row', 'col'), may hold values from 8 to 32, as said below
- link_tiles: float32 [32, 8, 8, 256, 256], P('row', 'col'), may hold values from -0.125 to 0.125
- link_rows: int32 [32, 8, 8], P('row', 'col'), may hold values from 0 to 63
- link_target: int32 [32, 8, 8], P('row', 'col'), may hold values from 0 to 7
- link_columns: int32 [8], replicated, may hold values from 0 to 2047, as said below
- objective: float32 [524288], P(('col', 'row')), may hold values from -16 to 16
- upper_bound: float32 [524288], P(('col', 'row')), may hold values from 0.25 to 4
- right_side: float32 [524288], P(('row', 'col')), may hold values from -16 to 16
- primal_start: float32 [524288], P(('col', 'row')), may hold values from 0 to 1
- dual_start: float32 [524288], P(('row', 'col')), may hold values from 0 to 1
- primal_weight: float32 [1], replicated, may hold values from 0.5 to 2
- step_start: float32 [1], replicated, may hold values from 2 to 4
Outputs:
- primal_out: float32 [524288], P(('col', 'row'))
- dual_out: float32 [524288], P(('row', 'col'))
- step_out: float32 [1], replicated
The draws below stay inside these ranges and needn't reach their ends.
Inputs may be any that keep to these rules, and one draw needn't show every extreme that they name: Slots 0 to tile_count - 1 of a device are live and the others are to be ignored; at least one device has all 32 slots live. `tile_rows`: the live slots of one device name distinct tiles. `tile_cols`: the live slots of one device name distinct tiles. `link_columns`: distinct column tiles; the first and the last column tile are always among them.
All inputs are finite; a program needn't handle non-finite values.
Results may differ from the reference program's by a relative error of at most 0.0003.
Values sent between devices are 32-bit elements; how exact they have to be, the bound alone decides.
A program may use at most 64 MiB of HBM per device.

```python
import math
import jax
import jax.numpy as jnp
from jax import lax

TILE = 256
RT = 64
CT = 256
SLOTS = 32
LSLOT = 8
LINK = 8
ITERS = 2
NROWS = 524288
NCOLS = 524288
N_ROW = 32
N_COL = 8


def tile_positions(key):
    device_keys = jax.random.split(jax.random.fold_in(key, 101), N_ROW * N_COL)

    def one_device(device_key):
        return jax.random.permutation(device_key, RT * CT)[:SLOTS]
    return jax.vmap(one_device)(device_keys).reshape(N_ROW, N_COL, SLOTS).astype(jnp.int32)


def draw_tile_rows(key, part):
    return (tile_positions(key) // CT).astype(jnp.int32)


def draw_tile_cols(key, part):
    return (tile_positions(key) % CT).astype(jnp.int32)


def draw_tile_count(key, part):
    first_key, second_key = jax.random.split(jax.random.fold_in(key, 202))
    counts = jax.random.randint(first_key, (N_ROW * N_COL,), SLOTS // 4, SLOTS + 1)
    fullest = jax.random.randint(second_key, (), 0, N_ROW * N_COL)
    return counts.at[fullest].set(SLOTS).reshape(N_ROW, N_COL).astype(jnp.int32)


def draw_link_columns(key, part):
    total = N_COL * CT
    scores = jax.random.randint(jax.random.fold_in(key, 3030), (total,), 0, 1 << 18)
    scores = scores.at[0].set(1 << 18).at[total - 1].set(1 << 18)
    distinct = scores * total + jnp.arange(total, dtype=jnp.int32)
    chosen = jax.lax.top_k(distinct, LINK)[1]
    return chosen.astype(jnp.int32)


def rising(key, length):
    position = jnp.arange(length, dtype=jnp.float32) / length
    spread_factor = 1.0 + 2.0 * position
    return jax.random.truncated_normal(key, -4.0, 4.0, (length,), jnp.float32) * spread_factor


def draw_objective(key, part):
    return rising(jax.random.fold_in(key, 404), NCOLS)


def draw_right_side(key, part):
    return rising(jax.random.fold_in(key, 505), NROWS)


def touch_ends(drawn, own_key, smallest, largest):
    spot = [jax.random.randint(jax.random.fold_in(own_key, axis), (), 0, length) for axis, length in enumerate(drawn.shape)]
    widest = drawn.shape.index(max(drawn.shape))
    beside = spot[:widest] + [(spot[widest] + 1) % drawn.shape[widest]] + spot[widest + 1:]
    return drawn.at[tuple(spot)].set(smallest).at[tuple(beside)].set(largest)


def block_levels(rng, extent, pieces, smallest, largest):
    gain = 1.0
    for dim, blocks in pieces:
        draws = jax.random.uniform(jax.random.fold_in(jax.random.fold_in(rng, 6), dim), (blocks,), jnp.float32, smallest / len(pieces), largest / len(pieces))
        gain = gain * jnp.repeat(jnp.exp(draws), extent[dim] // blocks).reshape((-1,) + (1,) * (len(extent) - 1 - dim))
    return gain


def centred(rng, shape, scale, reach, pieces=(), kind=jnp.bfloat16):
    entries = scale * jax.random.normal(rng, shape, jnp.float32)
    if pieces:
        entries = entries * block_levels(rng, shape, pieces, -0.22, 0.18)
    return jnp.clip(entries, -reach, reach).astype(kind)


def setup_inputs(seed: int = 0) -> dict:
    arg_keys = jax.random.split(jax.random.key(seed), 16)
    matrix_tiles = centred(arg_keys[0], (N_ROW, N_COL, SLOTS, TILE, TILE), (TILE * 2) ** -0.5, 0.25, ((0, 32), (1, 8)), jnp.float32)
    tile_rows = draw_tile_rows(jax.random.fold_in(arg_keys[15], 71), 0)
    tile_cols = draw_tile_cols(jax.random.fold_in(arg_keys[15], 71), 0)
    tile_count = draw_tile_count(jax.random.fold_in(arg_keys[15], 71), 0)
    link_tiles = centred(arg_keys[4], (N_ROW, N_COL, LSLOT, TILE, TILE), (TILE * 8) ** -0.5, 0.125, ((0, 32), (1, 8)), jnp.float32)
    link_rows = touch_ends(jax.random.randint(arg_keys[5], (N_ROW, N_COL, LSLOT), 0, RT), jax.random.fold_in(arg_keys[5], 1), 0, RT - 1).astype(jnp.int32)
    link_target = touch_ends(jax.random.randint(arg_keys[6], (N_ROW, N_COL, LSLOT), 0, LINK), jax.random.fold_in(arg_keys[6], 1), 0, LINK - 1).astype(jnp.int32)
    link_columns = draw_link_columns(jax.random.fold_in(arg_keys[15], 71), 0)
    objective = draw_objective(jax.random.fold_in(arg_keys[15], 71), 0)
    upper_bound = jnp.clip(jnp.exp(math.log(4.0) - 2.7725887 * jax.random.uniform(arg_keys[9], (NCOLS,), jnp.float32) ** block_levels(arg_keys[9], (NCOLS,), ((0, 256),), -0.2, 0.2)), 0.25, 4.0)
    right_side = draw_right_side(jax.random.fold_in(arg_keys[15], 71), 0)
    primal_start = jnp.clip(1.0 * jax.random.uniform(arg_keys[11], (NCOLS,), jnp.float32) ** block_levels(arg_keys[11], (NCOLS,), ((0, 256),), -0.2, 0.2), 0.0, 1.0)
    dual_start = jnp.clip(1.0 * jax.random.uniform(arg_keys[12], (NROWS,), jnp.float32) ** block_levels(arg_keys[12], (NROWS,), ((0, 256),), -0.2, 0.2), 0.0, 1.0)
    primal_weight = jnp.clip(jnp.exp(jax.random.uniform(arg_keys[13], (1,), jnp.float32, math.log(0.5), math.log(2.0))), 0.5, 2.0)
    step_start = jnp.clip(jax.random.uniform(arg_keys[14], (1,), jnp.float32, 2.0, 4.0), 2.0, 4.0)
    return {"matrix_tiles": matrix_tiles, "tile_rows": tile_rows, "tile_cols": tile_cols, "tile_count": tile_count, "link_tiles": link_tiles, "link_rows": link_rows, "link_target": link_target, "link_columns": link_columns, "objective": objective, "upper_bound": upper_bound, "right_side": right_side, "primal_start": primal_start, "dual_start": dual_start, "primal_weight": primal_weight, "step_start": step_start}


def apply_forward(matrix_tiles, tile_rows, tile_cols, slot_mask, link_tiles, link_rows, link_target, link_columns, vector_in):
    row_numbers = jnp.arange(N_ROW, dtype=jnp.int32)[:, None, None]
    col_numbers = jnp.arange(N_COL, dtype=jnp.int32)[None, :, None]
    vector_tiles = vector_in.reshape(N_COL, CT, TILE)
    picked = vector_tiles[col_numbers, tile_cols]
    products = jnp.einsum("rcsij,rcsj->rcsi", matrix_tiles, picked, precision=lax.Precision.HIGHEST) * slot_mask[:, :, :, None]
    result = jnp.zeros((N_ROW, RT, TILE), jnp.float32).at[row_numbers, tile_rows].add(products)
    link_values = vector_in.reshape(N_COL * CT, TILE)[link_columns]
    strip_picked = link_values[link_target]
    strip_products = jnp.einsum("rcsij,rcsj->rcsi", link_tiles, strip_picked, precision=lax.Precision.HIGHEST)
    result = result.at[row_numbers, link_rows].add(strip_products)
    return result.reshape(-1)


def apply_transpose(matrix_tiles, tile_rows, tile_cols, slot_mask, link_tiles, link_rows, link_target, link_columns, vector_in):
    row_numbers = jnp.arange(N_ROW, dtype=jnp.int32)[:, None, None]
    col_numbers = jnp.arange(N_COL, dtype=jnp.int32)[None, :, None]
    vector_tiles = vector_in.reshape(N_ROW, RT, TILE)
    picked = vector_tiles[row_numbers, tile_rows]
    products = jnp.einsum("rcsij,rcsi->rcsj", matrix_tiles, picked, precision=lax.Precision.HIGHEST) * slot_mask[:, :, :, None]
    result = jnp.zeros((N_COL, CT, TILE), jnp.float32).at[col_numbers, tile_cols].add(products)
    strip_picked = vector_tiles[row_numbers, link_rows]
    strip_products = jnp.einsum("rcsij,rcsi->rcsj", link_tiles, strip_picked, precision=lax.Precision.HIGHEST)
    link_sums = jnp.zeros((LINK, TILE), jnp.float32).at[link_target].add(strip_products)
    result = result.reshape(N_COL * CT, TILE).at[link_columns].add(link_sums)
    return result.reshape(-1)


def reference(matrix_tiles, tile_rows, tile_cols, tile_count, link_tiles, link_rows, link_target, link_columns, objective, upper_bound, right_side, primal_start, dual_start, primal_weight, step_start):
    slot_mask = (jnp.arange(SLOTS, dtype=jnp.int32)[None, None, :] < tile_count[:, :, None]).astype(jnp.float32)
    pattern = (matrix_tiles, tile_rows, tile_cols, slot_mask, link_tiles, link_rows, link_target, link_columns)
    weight_value = primal_weight[0]
    step_size = step_start[0]
    primal_now = primal_start
    dual_now = dual_start
    primal_image = apply_forward(*pattern, primal_now)
    dual_image = apply_transpose(*pattern, dual_now)
    for iteration in range(ITERS):
        primal_step = step_size / weight_value
        dual_step = step_size * weight_value
        primal_next = jnp.clip(primal_now - primal_step * (objective - dual_image), 0.0, upper_bound)
        image_next = apply_forward(*pattern, primal_next)
        dual_next = jnp.maximum(dual_now + dual_step * (right_side - 2.0 * image_next + primal_image), 0.0)
        primal_change = primal_next - primal_now
        dual_change = dual_next - dual_now
        primal_square = jnp.sum(primal_change * primal_change)
        dual_square = jnp.sum(dual_change * dual_change)
        cross_term = jnp.sum(dual_change * (image_next - primal_image))
        weighted = weight_value * primal_square + dual_square / weight_value + 1e-6
        shrink = 1.0 - (iteration + 2.0) ** (-0.3)
        growth = 1.0 + (iteration + 2.0) ** (-0.6)
        step_size = shrink * weighted / jnp.maximum(2.0 * jnp.abs(cross_term), shrink * weighted / (growth * step_size))
        if iteration + 1 < ITERS:
            dual_image = apply_transpose(*pattern, dual_next)
        primal_now = primal_next
        dual_now = dual_next
        primal_image = image_next
    return primal_now, dual_now, jnp.reshape(step_size, (1,))
```

```python
import functools

import jax
import jax.numpy as jnp
from jax import lax
from jax.experimental import pallas as pl
from jax.experimental.pallas import tpu as pltpu
from jax.sharding import PartitionSpec as P

MESH = pl.DeviceIdType.MESH
F32 = jnp.float32
BF16 = jnp.bfloat16

NR = 32
NC = 8
T = 256
SLOTS = 32
LS = 8
GROUPS = 5
OWN = 16
XR = NR * OWN
YR = NC * OWN

PHASES = (
    [f"y{k}" for k in range(2)]
    + [f"x{k}" for k in range(3)]
    + [f"pull{k}" for k in range(2)]
    + [f"strip{k}" for k in range(2)]
    + [f"tab{k}" for k in range(3)]
    + [f"image{k}" for k in range(3)]
    + ["sum_col", "sum_z", "sum_yx", "last_z", "last_yx"]
)
PH = {name: i for i, name in enumerate(PHASES)}
CHUNK = 4 * T
CHUNKS = GROUPS * 8 * T // CHUNK
EARLY = 5


def dot(a, b):
    return lax.dot_general(a, b, (((1,), (0,)), ((), ())), preferred_element_type=F32)


def dot_t(a, b):
    return lax.dot_general(a, b, (((1,), (1,)), ((), ())), preferred_element_type=F32)


def two_parts(v):
    big = v.astype(BF16)
    return big, (v - big.astype(F32)).astype(BF16)


def side_by_side(v):
    big, small = two_parts(v)
    return jnp.concatenate([big, small], axis=1)


def placed(table, v):
    big, small = two_parts(v)
    rest = (v - big.astype(F32) - small.astype(F32)).astype(BF16)
    return dot(table, big) + dot(table, small) + dot(table, rest)


def stacked(p):
    big = p.astype(BF16).astype(F32)
    small = p - big
    return jnp.concatenate(
        [big[:, :128], big[:, 128:], small[:, :128], small[:, 128:]], axis=0
    ).astype(BF16)


def kernel(
    tiles,
    links,
    trow,
    tcol,
    cnt,
    lrow,
    ltgt,
    lcol,
    obj,
    ub,
    rhs,
    x0,
    y0,
    pw,
    st,
    x_out,
    y_out,
    s_out,
    landing,
    local,
    vectors,
    hi,
    lo,
    x0g,
    xg,
    yg,
    xpart,
    xsum,
    ypart,
    ysum,
    tab_s,
    tab_r,
    strip_s,
    strip_r,
    tot_s,
    tot_r,
    my_ref,
    mx_ref,
    gy_ref,
    gx_ref,
    gl_ref,
    ly_ref,
    lt_ref,
    lm_ref,
    picked,
    made,
    load_sem,
    small_sem,
    send_sem,
    recv_sem,
):
    r = lax.axis_index("row")
    c = lax.axis_index("col")
    ry, rx, rz = r // 8, (r // 2) % 4, r % 2
    ch, cc = c // 2, c % 2

    def row_peer(d):
        dy, dx, dz = d // 8, (d // 2) % 4, d % 2
        return (((ry + dy) % 4) * 4 + (rx + dx) % 4) * 2 + (rz + dz) % 2, c

    def row_back(d):
        dy, dx, dz = d // 8, (d // 2) % 4, d % 2
        return (((4 - dy) % 4) * 4 + (4 - dx) % 4) * 2 + dz

    def col_peer(d):
        return r, ((ch + d // 2) % 4) * 2 + (cc + d % 2) % 2

    def side_peer(d):
        dz, e = d // 8, d % 8
        return (ry * 4 + rx) * 2 + (rz + dz) % 2, col_peer(e)[1]

    def col_back(d):
        return ((4 - d // 2) % 4) * 2 + d % 2

    def send(name, peer, d, src, dst):
        k = PH[name]
        pltpu.make_async_remote_copy(
            src_ref=src,
            dst_ref=dst,
            send_sem=send_sem.at[k],
            recv_sem=recv_sem.at[k],
            device_id=peer(d),
            device_id_type=MESH,
        ).start()

    def send_all(name, peer, count, src_of, dst_of):
        def one(d, carry):
            send(name, peer, d, src_of(d), dst_of(d))
            return carry

        lax.fori_loop(1, count, one, 0)

    def slot(d, rows=OWN):
        return pl.ds(pl.multiple_of(d * rows, rows), rows)

    def total(name, ref):
        k = PH[name]
        return pltpu.make_async_remote_copy(
            src_ref=ref,
            dst_ref=ref,
            send_sem=send_sem.at[k],
            recv_sem=recv_sem.at[k],
            device_id=col_peer(1),
            device_id_type=MESH,
        )

    def arrived(name, ref):
        total(name, ref).wait_recv()

    pending = []

    barrier = pltpu.get_barrier_semaphore()
    def greet(peer):
        def one(d, carry):
            pl.semaphore_signal(barrier, inc=1, device_id=peer(d), device_id_type=MESH)
            return carry

        return one

    lax.fori_loop(1, 2 * NC, greet(side_peer), 0)
    lax.fori_loop(2, NR, greet(row_peer), 0)

    far = (y0, x0, ub, trow, tcol, cnt, lrow, ltgt, lcol, obj, rhs, pw, st)
    near = (
        yg.at[0, :OWN],
        x0g.at[0, :OWN],
        vectors.at[1],
        *local[:6],
        vectors.at[0],
        vectors.at[2],
        *local[6:],
    )
    small = [
        pltpu.make_async_copy(a, b, small_sem.at[i]) for i, (a, b) in enumerate(zip(far, near))
    ]
    for copy in small:
        copy.start()
    trow, tcol, cnt, lrow, ltgt, lcol, pw, st = local
    obj, ub, rhs = (vectors.at[i] for i in range(3))

    def load(i):
        rows = pl.ds(i * CHUNK, CHUNK)
        near_links = i * CHUNK - SLOTS * T
        src = tiles.at[rows] if near_links < 0 else links.at[pl.ds(near_links, CHUNK)]
        return pltpu.make_async_copy(src, landing.at[rows], load_sem.at[i])

    for i in range(EARLY):
        load(i).start()

    pl.semaphore_wait(barrier, 2 * NC + NR - 3)

    def gather_y(k, values=None):
        if values is not None:
            yg[k, :OWN] = values
        send_all(
            f"y{k}", col_peer, NC, lambda d: yg.at[k, :OWN], lambda d: yg.at[k, slot(col_back(d))]
        )
        pending.append((f"y{k}", yg.at[k, pl.ds(OWN, YR - OWN)]))

    def gather_x(k, values=None):
        if values is not None:
            xg[k, :OWN] = values
        send_all(
            f"x{k}", row_peer, NR, lambda d: xg.at[k, :OWN], lambda d: xg.at[k, slot(row_back(d))]
        )
        pending.append((f"x{k}", xg.at[k, pl.ds(OWN, XR - OWN)]))

    small[0].wait()
    gather_y(0)
    for i in range(EARLY, CHUNKS):
        load(i).start()

    def lanes(rows, count):
        shape = (rows, 4 * count)
        lane = lax.broadcasted_iota(jnp.int32, shape, 1)
        return lax.broadcasted_iota(jnp.int32, shape, 0), lane % count, (lane // count) % 2

    def four(v):
        return jnp.concatenate([v, v, v, v], axis=1)

    def dual_place(t):
        o = t >> 3
        rel = ((((o >> 1) - ch) & 3) << 1) | ((o - cc) & 1)
        return (rel << 3) | (t & 7)

    def primal_place(t):
        o = t >> 3
        rel = (
            ((((o >> 3) - ry) & 3) << 3) | ((((o >> 1) - rx) & 3) << 1) | ((o - rz) & 1)
        )
        return (rel << 3) | (t & 7)

    def one_hot(cond):
        return jnp.where(cond, 1.0, 0.0).astype(F32)

    for copy in small[1:]:
        copy.wait()
    row, s, h = lanes(XR, LS)
    spot = lcol[...] - c * (XR // 2)
    mine = (spot >= 0) & (spot < XR // 2)
    own = one_hot(row == 2 * four(jnp.where(mine, primal_place(spot), -8)) + h)
    own_here = jnp.transpose(own[:128])[: 2 * LS, :OWN].astype(BF16)
    x0g[0, OWN:] = placed(own_here, ub[...])
    send_all("x0", row_peer, NR, lambda d: x0g.at[0], lambda d: x0g.at[row_back(d)])
    pending.append(("x0", x0g.at[pl.ds(1, NR - 1)]))

    live = cnt[...]
    row, s, h = lanes(YR, SLOTS)
    my = one_hot((row == 2 * four(dual_place(trow[...])) + h) & (s < live))
    row, s, h = lanes(YR, LS)
    ly = one_hot(row == 2 * four(dual_place(lrow[...])) + h)
    row, s, h = lanes(XR, SLOTS)
    mx = one_hot((row == 2 * four(primal_place(tcol[...])) + h) & (s < live))
    own_pick = jnp.transpose(own)[: 2 * LS]
    own_pick_b = own_pick.astype(BF16)
    mx_b = mx.astype(BF16)
    both_here = dot(own_pick_b, mx_b)
    not_link = 1.0 - jnp.sum(own_pick, axis=0, keepdims=True)
    my_ref[...] = my.astype(BF16)
    mx_ref[...] = mx_b
    gy_ref[: 2 * SLOTS] = jnp.transpose(my)[: 2 * SLOTS].astype(BF16)
    gy_ref[2 * SLOTS :] = jnp.transpose(ly)[: 2 * LS].astype(BF16)
    gx_ref[: 2 * SLOTS] = (jnp.transpose(mx)[: 2 * SLOTS] * not_link).astype(BF16)
    gx_ref[2 * SLOTS :] = own_pick_b
    ly_ref[...] = ly.astype(BF16)
    row, s, h = lanes(2 * LS, LS)
    lt = one_hot(row == h * LS + four(ltgt[...]))
    gl_ref[: 2 * SLOTS] = jnp.transpose(both_here)[: 2 * SLOTS].astype(BF16)
    gl_ref[2 * SLOTS :] = jnp.transpose(lt)[: 2 * LS].astype(BF16)
    lt_ref[...] = lt.astype(BF16)
    lm_ref[...] = both_here.astype(BF16)
    here = own[:OWN, : 2 * LS].astype(BF16)
    link_row = jnp.sum(own[:OWN, : 2 * LS], axis=1, keepdims=True) > 0.0
    obj_link = placed(own_here, obj[...])

    for i in range(CHUNKS):
        load(i).wait()

        def split_tile(t, carry, i=i):
            rows = pl.ds(pl.multiple_of(i * CHUNK + t * T, T), T)
            big, small = two_parts(landing[rows])
            hi[rows] = big
            lo[rows] = small
            return carry

        lax.fori_loop(0, CHUNK // T, split_tile, 0)

    member = lax.broadcasted_iota(jnp.int32, (16, T), 0) % 8

    def halves(picks, count):
        left, right = picks[:count], picks[count:]
        big = jnp.concatenate([left[:, :128], right[:, :128]], axis=1)
        small = jnp.concatenate([left[:, 128:], right[:, 128:]], axis=1)
        return big, small

    def group(g, both, product):
        out = jnp.zeros((16, T), F32)
        for k in range(8):
            one = jnp.where(member == k, both, 0.0).astype(BF16)
            rows = pl.ds(pl.multiple_of((g * 8 + k) * T, T), T)
            out = out + product(one, hi[rows]) + product(one, lo[rows])
        return out[:8] + out[8:]

    def link_group(picks, product):
        return group(GROUPS - 1, jnp.concatenate(halves(picks, LS), axis=0), product)

    def main_groups(picks, product):
        big, small = halves(picks, SLOTS)
        for g in range(GROUPS - 1):
            picked[g, :8] = big[8 * g : 8 * g + 8]
            picked[g, 8:] = small[8 * g : 8 * g + 8]

        def one(g, carry):
            made[g] = group(g, picked[g], product)
            return carry

        lax.fori_loop(0, GROUPS - 1, one, 0)
        return made[...].reshape(SLOTS, T)

    def sum_slots(ref, k, first, slots):
        out = first
        for d in range(1, slots):
            out = out + ref[k, d * OWN : (d + 1) * OWN]
        return out

    def transpose_product(k, at_start=lambda: None, at_sent=lambda: None):
        arrived(f"y{k}", yg.at[k, pl.ds(OWN, YR - OWN)])
        at_start()
        picks = dot(gy_ref[...], side_by_side(yg[k]))
        main = stacked(main_groups(picks[: 2 * SLOTS], dot))
        xpart[k] = dot(mx_ref[...], main)
        send_all(
            f"pull{k}", row_peer, NR, lambda d: xpart.at[k, slot(d)], lambda d: xsum.at[k, slot(d)]
        )
        pending.append((f"pull{k}", xsum.at[k, pl.ds(OWN, XR - OWN)]))
        at_sent()
        link = stacked(link_group(picks[2 * SLOTS :], dot))
        strip_s[k] = dot(lt_ref[...], link) + dot(lm_ref[...], main) - obj_link
        send_all(
            f"strip{k}", row_peer, NR, lambda d: strip_s.at[k], lambda d: strip_r.at[k, slot(d)]
        )
        pending.append((f"strip{k}", strip_r.at[k, pl.ds(OWN, XR - OWN)]))

    def pull(k):
        arrived(f"pull{k}", xsum.at[k, pl.ds(OWN, XR - OWN)])
        return sum_slots(xsum, k, xpart[k, :OWN], NR)

    def share_table(k, table):
        tab_s[k][...] = table
        send_all(f"tab{k}", col_peer, NC, lambda d: tab_s[k], lambda d: tab_r[k].at[d])
        pending.append((f"tab{k}", tab_r[k].at[pl.ds(1, NC - 1)]))

    def shared_table(k):
        arrived(f"tab{k}", tab_r[k].at[pl.ds(1, NC - 1)])
        table = tab_s[k][...]
        for d in range(1, NC):
            table = table + tab_r[k][d]
        return table

    def share_links(k):
        arrived(f"strip{k}", strip_r.at[k, pl.ds(OWN, XR - OWN)])
        share_table(k + 1, sum_slots(strip_r, k, strip_s[k], NR))

    def link_pull(k):
        share_links(k)
        return shared_table(k + 1)

    def from_links(table):
        picks = dot(gl_ref[...], side_by_side(table))
        link = link_group(picks[2 * SLOTS :], dot_t)
        return picks[: 2 * SLOTS], dot(ly_ref[...], stacked(link))

    def forward_product(k, vector, picks, strips):
        picks = picks + dot(gx_ref[: 2 * SLOTS], side_by_side(vector))
        main = dot(my_ref[...], stacked(main_groups(picks, dot_t)))
        ypart[k] = main + strips
        send_all(
            f"image{k}", col_peer, NC, lambda d: ypart.at[k, slot(d)], lambda d: ysum.at[k, slot(d)]
        )
        pending.append((f"image{k}", ysum.at[k, pl.ds(OWN, YR - OWN)]))

    def gathered_x(k):
        arrived(f"x{k}", xg.at[k, pl.ds(OWN, XR - OWN)])
        return xg[k]

    def image(k):
        arrived(f"image{k}", ysum.at[k, pl.ds(OWN, YR - OWN)])
        return sum_slots(ysum, k, ypart[k, :OWN], NC)

    weight = pw[...]
    step = st[...]

    def next_primal(now, step, pulled):
        return jnp.clip(now - (step / weight) * (obj[...] - pulled), 0.0, ub[...])

    def next_dual(now, step, old, new):
        return jnp.maximum(now + (step * weight) * (rhs[...] - 2.0 * new + old), 0.0)

    def sums(dx, dy, di):
        rows = [jnp.sum(v, axis=0, keepdims=True) for v in (dx * dx, dy * dy, dy * di)]
        return jnp.concatenate(rows + [jnp.zeros((5, 128), F32)], axis=0)

    def spread(name, first, value, peers, src):
        peer, count = peers
        tot_s[src] = value
        send_all(
            name, peer, count, lambda d: tot_s.at[src], lambda d: tot_r.at[slot(first + d - 1, 8)]
        )
        pending.append((name, tot_r.at[pl.ds(first * 8, (count - 1) * 8)]))

    def collect(name, first, value, count):
        arrived(name, tot_r.at[pl.ds(first * 8, count * 8)])
        for i in range(count):
            value = value + tot_r[(first + i) * 8 : (first + i + 1) * 8]
        return value

    col_peers = (col_peer, NC)
    z_peers = (row_peer, 2)
    yx_peers = (lambda d: row_peer(2 * d), NR // 2)
    side_peers = (side_peer, 2 * NC)

    def next_step(step, totals, iteration):
        lanes_summed = jnp.sum(totals, axis=1, keepdims=True)
        primal, dual, cross = lanes_summed[0:1], lanes_summed[1:2], lanes_summed[2:3]
        weighted = weight * primal + dual / weight + 1e-6
        shrink = 1.0 - (iteration + 2.0) ** (-0.3)
        growth = 1.0 + (iteration + 2.0) ** (-0.6)
        return (
            shrink
            * weighted
            / jnp.maximum(2.0 * jnp.abs(cross), shrink * weighted / (growth * step))
        )

    transpose_product(0)
    arrived("x0", x0g.at[pl.ds(1, NR - 1)])
    start = x0g[...]
    vector = start[:, :OWN].reshape(XR, 128)
    table = dot(own_pick_b, side_by_side(vector))
    share_table(
        0,
        jnp.concatenate([table[:, :128] + table[:, 128:], jnp.sum(start[:, OWN:], axis=0)], 0),
    )

    def next_links(now, step, pulled):
        return jnp.clip(now + (step / weight) * pulled, 0.0, ub_link)

    def patched(x, links):
        return jnp.where(link_row, placed(here, links), x)

    x_now = x0g[0, :OWN]
    y_now = yg[0, :OWN]
    x_next = next_primal(x_now, step, pull(0))
    gather_x(1, x_next)
    table = shared_table(0)
    x_link, ub_link = table[:OWN], table[OWN:]
    share_links(0)
    forward_product(0, vector, *from_links(x_link))
    x_link = next_links(x_link, step, shared_table(1))
    beside = from_links(x_link)
    x_next = patched(x_next, x_link)
    forward_product(1, gathered_x(1), *beside)
    image_old = image(0)
    image_new = image(1)
    y_next = next_dual(y_now, step, image_old, image_new)
    gather_y(1, y_next)
    value = sums(x_next - x_now, y_next - y_now, image_new - image_old)
    spread("sum_col", 0, value, col_peers, 0)
    x_now, y_now, image_old = x_next, y_next, image_new

    def at_start():
        spread("sum_z", 7, collect("sum_col", 0, value, 7), z_peers, 1)

    def at_sent():
        spread("sum_yx", 8, collect("sum_z", 7, tot_s[1], 1), yx_peers, 2)

    transpose_product(1, at_start, at_sent)
    step = next_step(step, collect("sum_yx", 8, tot_s[2], 15), 0)
    x_next = next_primal(x_now, step, pull(1))
    gather_x(2, x_next)
    x_link = next_links(x_link, step, link_pull(1))
    beside = from_links(x_link)
    x_next = patched(x_next, x_link)
    x_out[...] = x_next
    forward_product(2, gathered_x(2), *beside)
    image_new = image(2)
    y_next = next_dual(y_now, step, image_old, image_new)
    y_out[...] = y_next
    value = sums(x_next - x_now, y_next - y_now, image_new - image_old)
    spread("last_z", 23, value, side_peers, 3)
    value = collect("last_z", 23, value, 15)
    spread("last_yx", 38, value, yx_peers, 4)
    value = collect("last_yx", 38, value, 15)
    s_out[...] = next_step(step, value, 1)

    for name, ref in pending:
        total(name, ref).wait_send()


def on_device(
    matrix_tiles,
    tile_rows,
    tile_cols,
    tile_count,
    link_tiles,
    link_rows,
    link_target,
    link_columns,
    objective,
    upper_bound,
    right_side,
    primal_start,
    dual_start,
    primal_weight,
    step_start,
):
    flat = lambda v: v.reshape(OWN, 128)
    vmem = pl.BlockSpec(memory_space=pltpu.VMEM)
    hbm = pl.BlockSpec(memory_space=pltpu.HBM)
    n = len(PHASES)
    x, y, s = pl.pallas_call(
        kernel,
        out_shape=(
            jax.ShapeDtypeStruct((OWN, 128), F32),
            jax.ShapeDtypeStruct((OWN, 128), F32),
            jax.ShapeDtypeStruct((1, 1), F32),
        ),
        in_specs=[hbm] * 15,
        out_specs=(vmem, vmem, vmem),
        scratch_shapes=[
            pltpu.VMEM((GROUPS * 8 * T, T), F32),
            [pltpu.VMEM((1, m), jnp.int32) for m in (SLOTS, SLOTS, 1, LS, LS, LS)]
            + [pltpu.VMEM((1, 1), F32)] * 2,
            pltpu.VMEM((3, OWN, 128), F32),
            pltpu.VMEM((GROUPS * 8 * T, T), BF16),
            pltpu.VMEM((GROUPS * 8 * T, T), BF16),
            pltpu.VMEM((NR, 2 * OWN, 128), F32),
            pltpu.VMEM((3, XR, 128), F32),
            pltpu.VMEM((2, YR, 128), F32),
            pltpu.VMEM((2, XR, 128), F32),
            pltpu.VMEM((2, XR, 128), F32),
            pltpu.VMEM((3, YR, 128), F32),
            pltpu.VMEM((3, YR, 128), F32),
            [pltpu.VMEM((m * OWN, 128), F32) for m in (2, 1, 1)],
            [pltpu.VMEM((NC, m * OWN, 128), F32) for m in (2, 1, 1)],
            pltpu.VMEM((2, OWN, 128), F32),
            pltpu.VMEM((2, XR, 128), F32),
            pltpu.VMEM((5, 8, 128), F32),
            pltpu.VMEM((53 * 8, 128), F32),
            pltpu.VMEM((YR, 128), BF16),
            pltpu.VMEM((XR, 128), BF16),
            pltpu.VMEM((80, YR), BF16),
            pltpu.VMEM((80, XR), BF16),
            pltpu.VMEM((80, 16), BF16),
            pltpu.VMEM((YR, 32), BF16),
            pltpu.VMEM((16, 32), BF16),
            pltpu.VMEM((16, 128), BF16),
            pltpu.VMEM((GROUPS - 1, 16, T), F32),
            pltpu.VMEM((GROUPS - 1, 8, T), F32),
            pltpu.SemaphoreType.DMA((CHUNKS,)),
            pltpu.SemaphoreType.DMA((13,)),
            pltpu.SemaphoreType.DMA((n,)),
            pltpu.SemaphoreType.DMA((n,)),
        ],
        compiler_params=pltpu.CompilerParams(
            collective_id=0, has_side_effects=True, vmem_limit_bytes=63 * 1024 * 1024
        ),
        name="pdhg",
    )(
        matrix_tiles.reshape(SLOTS * T, T),
        link_tiles.reshape(LS * T, T),
        tile_rows.reshape(1, SLOTS),
        tile_cols.reshape(1, SLOTS),
        tile_count.reshape(1, 1),
        link_rows.reshape(1, LS),
        link_target.reshape(1, LS),
        link_columns.reshape(1, LS),
        flat(objective),
        flat(upper_bound),
        flat(right_side),
        flat(primal_start),
        flat(dual_start),
        primal_weight.reshape(1, 1),
        step_start.reshape(1, 1),
    )
    return x.reshape(-1), y.reshape(-1), s.reshape(1)


def solution(mesh):
    tile = P("row", "col", None, None, None)
    index = P("row", "col", None)
    primal = P(("col", "row"))
    dual = P(("row", "col"))
    return jax.shard_map(
        on_device,
        mesh=mesh,
        in_specs=(
            tile,
            index,
            index,
            P("row", "col"),
            tile,
            index,
            index,
            P(),
            primal,
            primal,
            dual,
            primal,
            dual,
            P(),
            P(),
        ),
        out_specs=(primal, dual, P()),
        check_vma=False,
    )
```

```python
import functools

import jax
import jax.numpy as jnp
from jax import lax
from jax.experimental import pallas as pl
from jax.experimental.pallas import tpu as pltpu
from jax.sharding import PartitionSpec as P

MESH = pl.DeviceIdType.MESH
F32 = jnp.float32
BF16 = jnp.bfloat16

NR = 32
NC = 8
T = 256
SLOTS = 32
LS = 8
GROUPS = 5
OWN = 16
XR = NR * OWN
YR = NC * OWN

PHASES = (
    [f"y{k}" for k in range(2)]
    + [f"x{k}" for k in range(3)]
    + [f"pull{k}" for k in range(2)]
    + [f"strip{k}" for k in range(2)]
    + [f"tab{k}" for k in range(3)]
    + [f"image{k}" for k in range(3)]
    + ["sum_col", "sum_row", "last_z", "last_yx"]
)
PH = {name: i for i, name in enumerate(PHASES)}
CHUNK = 4 * T
CHUNKS = GROUPS * 8 * T // CHUNK
EARLY = 5


def dot(a, b):
    return lax.dot_general(a, b, (((1,), (0,)), ((), ())), preferred_element_type=F32)


def two_parts(v):
    big = v.astype(BF16)
    return big, (v - big.astype(F32)).astype(BF16)


def side_by_side(v):
    big, small = two_parts(v)
    return jnp.concatenate([big, small], axis=1)


def placed(table, v):
    big, small = two_parts(v)
    rest = (v - big.astype(F32) - small.astype(F32)).astype(BF16)
    return dot(table, big) + dot(table, small) + dot(table, rest)


def stacked(p):
    big = p.astype(BF16).astype(F32)
    small = p - big
    return jnp.concatenate(
        [big[:, :128], big[:, 128:], small[:, :128], small[:, 128:]], axis=0
    ).astype(BF16)


def kernel(
    tiles,
    links,
    trow,
    tcol,
    cnt,
    lrow,
    ltgt,
    lcol,
    obj,
    ub,
    rhs,
    x0,
    y0,
    pw,
    st,
    x_out,
    y_out,
    s_out,
    landing,
    local,
    vectors,
    hi,
    lo,
    hi_t,
    lo_t,
    x0g,
    xg,
    yg,
    xpart,
    xsum,
    ypart,
    ysum,
    tab_s,
    tab_r,
    strip_s,
    strip_r,
    tot_s,
    tot_r,
    my_ref,
    mx_ref,
    gy_ref,
    gx_ref,
    gl_ref,
    ly_ref,
    lt_ref,
    lm_ref,
    picked,
    made,
    results,
    load_sem,
    small_sem,
    send_sem,
    recv_sem,
):
    r = lax.axis_index("row")
    c = lax.axis_index("col")
    ry, rx, rz = r // 8, (r // 2) % 4, r % 2
    ch, cc = c // 2, c % 2

    def row_peer(d):
        dy, dx, dz = d // 8, (d // 2) % 4, d % 2
        return (((ry + dy) % 4) * 4 + (rx + dx) % 4) * 2 + (rz + dz) % 2, c

    def row_back(d):
        dy, dx, dz = d // 8, (d // 2) % 4, d % 2
        return (((4 - dy) % 4) * 4 + (4 - dx) % 4) * 2 + dz

    def col_peer(d):
        return r, ((ch + d // 2) % 4) * 2 + (cc + d % 2) % 2

    def side_peer(d):
        dz, e = d // 8, d % 8
        return (ry * 4 + rx) * 2 + (rz + dz) % 2, col_peer(e)[1]

    def col_back(d):
        return ((4 - d // 2) % 4) * 2 + d % 2

    def send(name, peer, d, src, dst):
        k = PH[name]
        pltpu.make_async_remote_copy(
            src_ref=src,
            dst_ref=dst,
            send_sem=send_sem.at[k],
            recv_sem=recv_sem.at[k],
            device_id=peer(d),
            device_id_type=MESH,
        ).start()

    def send_all(name, peer, count, src_of, dst_of):
        def one(d, carry):
            send(name, peer, d, src_of(d), dst_of(d))
            return carry

        lax.fori_loop(1, count, one, 0)

    def slot(d, rows=OWN):
        return pl.ds(pl.multiple_of(d * rows, rows), rows)

    def total(name, ref):
        k = PH[name]
        return pltpu.make_async_remote_copy(
            src_ref=ref,
            dst_ref=ref,
            send_sem=send_sem.at[k],
            recv_sem=recv_sem.at[k],
            device_id=col_peer(1),
            device_id_type=MESH,
        )

    def arrived(name, ref):
        total(name, ref).wait_recv()

    pending = []

    barrier = pltpu.get_barrier_semaphore()
    def greet(peer):
        def one(d, carry):
            pl.semaphore_signal(barrier, inc=1, device_id=peer(d), device_id_type=MESH)
            return carry

        return one

    lax.fori_loop(1, 2 * NC, greet(side_peer), 0)
    lax.fori_loop(2, NR, greet(row_peer), 0)

    far = (y0, x0, ub, trow, tcol, cnt, lrow, ltgt, lcol, obj, rhs, pw, st)
    near = (
        yg.at[0, :OWN],
        x0g.at[0, :OWN],
        vectors.at[1],
        *local[:6],
        vectors.at[0],
        vectors.at[2],
        *local[6:],
    )
    small = [
        pltpu.make_async_copy(a, b, small_sem.at[i]) for i, (a, b) in enumerate(zip(far, near))
    ]
    for copy in small:
        copy.start()
    trow, tcol, cnt, lrow, ltgt, lcol, pw, st = local
    obj, ub, rhs = (vectors.at[i] for i in range(3))

    def load(i):
        rows = pl.ds(i * CHUNK, CHUNK)
        near_links = i * CHUNK - SLOTS * T
        src = tiles.at[rows] if near_links < 0 else links.at[pl.ds(near_links, CHUNK)]
        return pltpu.make_async_copy(src, landing.at[rows], load_sem.at[i])

    for i in range(EARLY):
        load(i).start()

    pl.semaphore_wait(barrier, 2 * NC + NR - 3)

    def gather_y(k, values=None):
        if values is not None:
            yg[k, :OWN] = values
        send_all(
            f"y{k}", col_peer, NC, lambda d: yg.at[k, :OWN], lambda d: yg.at[k, slot(col_back(d))]
        )
        pending.append((f"y{k}", yg.at[k, pl.ds(OWN, YR - OWN)]))

    def gather_x(k, values=None):
        if values is not None:
            xg[k, :OWN] = values
        send_all(
            f"x{k}", row_peer, NR, lambda d: xg.at[k, :OWN], lambda d: xg.at[k, slot(row_back(d))]
        )
        pending.append((f"x{k}", xg.at[k, pl.ds(OWN, XR - OWN)]))

    small[0].wait()
    gather_y(0)
    for i in range(EARLY, CHUNKS):
        load(i).start()

    def lanes(rows, count):
        shape = (rows, 4 * count)
        lane = lax.broadcasted_iota(jnp.int32, shape, 1)
        return lax.broadcasted_iota(jnp.int32, shape, 0), lane % count, (lane // count) % 2

    def four(v):
        return jnp.concatenate([v, v, v, v], axis=1)

    def dual_place(t):
        o = t >> 3
        rel = ((((o >> 1) - ch) & 3) << 1) | ((o - cc) & 1)
        return (rel << 3) | (t & 7)

    def primal_place(t):
        o = t >> 3
        rel = (
            ((((o >> 3) - ry) & 3) << 3) | ((((o >> 1) - rx) & 3) << 1) | ((o - rz) & 1)
        )
        return (rel << 3) | (t & 7)

    def one_hot(cond):
        return jnp.where(cond, 1.0, 0.0).astype(F32)

    for copy in small[1:]:
        copy.wait()
    row, s, h = lanes(XR, LS)
    spot = lcol[...] - c * (XR // 2)
    mine = (spot >= 0) & (spot < XR // 2)
    own = one_hot(row == 2 * four(jnp.where(mine, primal_place(spot), -8)) + h)
    own_here = jnp.transpose(own[:128])[: 2 * LS, :OWN].astype(BF16)
    x0g[0, OWN:] = placed(own_here, ub[...])
    send_all("x0", row_peer, NR, lambda d: x0g.at[0], lambda d: x0g.at[row_back(d)])
    pending.append(("x0", x0g.at[pl.ds(1, NR - 1)]))

    live = cnt[...]
    row, s, h = lanes(YR, SLOTS)
    my = one_hot((row == 2 * four(dual_place(trow[...])) + h) & (s < live))
    row, s, h = lanes(YR, LS)
    ly = one_hot(row == 2 * four(dual_place(lrow[...])) + h)
    row, s, h = lanes(XR, SLOTS)
    mx = one_hot((row == 2 * four(primal_place(tcol[...])) + h) & (s < live))
    own_pick = jnp.transpose(own)[: 2 * LS]
    own_pick_b = own_pick.astype(BF16)
    mx_b = mx.astype(BF16)
    both_here = dot(own_pick_b, mx_b)
    not_link = 1.0 - jnp.sum(own_pick, axis=0, keepdims=True)
    my_ref[...] = my.astype(BF16)
    mx_ref[...] = mx_b
    gy_ref[: 2 * SLOTS] = jnp.transpose(my)[: 2 * SLOTS].astype(BF16)
    gy_ref[2 * SLOTS :] = jnp.transpose(ly)[: 2 * LS].astype(BF16)
    gx_ref[: 2 * SLOTS] = (jnp.transpose(mx)[: 2 * SLOTS] * not_link).astype(BF16)
    gx_ref[2 * SLOTS :] = own_pick_b
    ly_ref[...] = ly.astype(BF16)
    row, s, h = lanes(2 * LS, LS)
    lt = one_hot(row == h * LS + four(ltgt[...]))
    gl_ref[: 2 * SLOTS] = jnp.transpose(both_here)[: 2 * SLOTS].astype(BF16)
    gl_ref[2 * SLOTS :] = jnp.transpose(lt)[: 2 * LS].astype(BF16)
    lt_ref[...] = lt.astype(BF16)
    lm_ref[...] = both_here.astype(BF16)
    here = own[:OWN, : 2 * LS].astype(BF16)
    link_row = jnp.sum(own[:OWN, : 2 * LS], axis=1, keepdims=True) > 0.0
    obj_link = placed(own_here, obj[...])

    for i in range(CHUNKS):
        load(i).wait()

        def split_tile(t, carry, i=i):
            rows = pl.ds(pl.multiple_of(i * CHUNK + t * T, T), T)
            big, small = two_parts(landing[rows])
            hi[rows] = big
            lo[rows] = small
            return carry

        lax.fori_loop(0, CHUNK // T, split_tile, 0)

    member = lax.broadcasted_iota(jnp.int32, (16, T), 0) % 8

    def halves(picks, count):
        left, right = picks[:count], picks[count:]
        big = jnp.concatenate([left[:, :128], right[:, :128]], axis=1)
        small = jnp.concatenate([left[:, 128:], right[:, 128:]], axis=1)
        return big, small

    def group(g, both, parts):
        out = jnp.zeros((16, T), F32)
        for k in range(8):
            one = jnp.where(member == k, both, 0.0).astype(BF16)
            rows = pl.ds(pl.multiple_of((g * 8 + k) * T, T), T)
            out = out + dot(one, parts[0][rows]) + dot(one, parts[1][rows])
        return out[:8] + out[8:]

    def link_group(picks, parts):
        return group(GROUPS - 1, jnp.concatenate(halves(picks, LS), axis=0), parts)

    def main_groups(picks, parts):
        big, small = halves(picks, SLOTS)
        for g in range(GROUPS - 1):
            picked[g, :8] = big[8 * g : 8 * g + 8]
            picked[g, 8:] = small[8 * g : 8 * g + 8]

        def one(g, carry):
            made[g] = group(g, picked[g], parts)
            return carry

        lax.fori_loop(0, GROUPS - 1, one, 0)
        return made[...].reshape(SLOTS, T)

    def sum_slots(ref, k, first, slots):
        out = first
        for d in range(1, slots):
            out = out + ref[k, d * OWN : (d + 1) * OWN]
        return out

    def transpose_product(k, at_start=lambda: None):
        arrived(f"y{k}", yg.at[k, pl.ds(OWN, YR - OWN)])
        at_start()
        picks = dot(gy_ref[...], side_by_side(yg[k]))
        main = stacked(main_groups(picks[: 2 * SLOTS], (hi, lo)))
        xpart[k] = dot(mx_ref[...], main)
        send_all(
            f"pull{k}", row_peer, NR, lambda d: xpart.at[k, slot(d)], lambda d: xsum.at[k, slot(d)]
        )
        pending.append((f"pull{k}", xsum.at[k, pl.ds(OWN, XR - OWN)]))
        link = stacked(link_group(picks[2 * SLOTS :], (hi, lo)))
        strip_s[k] = dot(lt_ref[...], link) + dot(lm_ref[...], main) - obj_link
        send_all(
            f"strip{k}", row_peer, NR, lambda d: strip_s.at[k], lambda d: strip_r.at[k, slot(d)]
        )
        pending.append((f"strip{k}", strip_r.at[k, pl.ds(OWN, XR - OWN)]))

    def pull(k):
        arrived(f"pull{k}", xsum.at[k, pl.ds(OWN, XR - OWN)])
        return sum_slots(xsum, k, xpart[k, :OWN], NR)

    def share_table(k, table):
        tab_s[k][...] = table
        send_all(f"tab{k}", col_peer, NC, lambda d: tab_s[k], lambda d: tab_r[k].at[d])
        pending.append((f"tab{k}", tab_r[k].at[pl.ds(1, NC - 1)]))

    def shared_table(k):
        arrived(f"tab{k}", tab_r[k].at[pl.ds(1, NC - 1)])
        table = tab_s[k][...]
        for d in range(1, NC):
            table = table + tab_r[k][d]
        return table

    def share_links(k):
        arrived(f"strip{k}", strip_r.at[k, pl.ds(OWN, XR - OWN)])
        share_table(k + 1, sum_slots(strip_r, k, strip_s[k], NR))

    def link_pull(k):
        share_links(k)
        return shared_table(k + 1)

    def from_links(table):
        picks = dot(gl_ref[...], side_by_side(table))
        link = link_group(picks[2 * SLOTS :], (hi_t, lo_t))
        return picks[: 2 * SLOTS], dot(ly_ref[...], stacked(link))

    def forward_product(k, vector, picks, strips):
        picks = picks + dot(gx_ref[: 2 * SLOTS], side_by_side(vector))
        main = dot(my_ref[...], stacked(main_groups(picks, (hi_t, lo_t))))
        ypart[k] = main + strips
        send_all(
            f"image{k}", col_peer, NC, lambda d: ypart.at[k, slot(d)], lambda d: ysum.at[k, slot(d)]
        )
        pending.append((f"image{k}", ysum.at[k, pl.ds(OWN, YR - OWN)]))

    def gathered_x(k):
        arrived(f"x{k}", xg.at[k, pl.ds(OWN, XR - OWN)])
        return xg[k]

    def image(k):
        arrived(f"image{k}", ysum.at[k, pl.ds(OWN, YR - OWN)])
        return sum_slots(ysum, k, ypart[k, :OWN], NC)

    weight = pw[...]
    step = st[...]

    def next_primal(now, step, pulled):
        return jnp.clip(now - (step / weight) * (obj[...] - pulled), 0.0, ub[...])

    def next_dual(now, step, old, new):
        return jnp.maximum(now + (step * weight) * (rhs[...] - 2.0 * new + old), 0.0)

    def sums(dx, dy, di):
        rows = [jnp.sum(v, axis=0, keepdims=True) for v in (dx * dx, dy * dy, dy * di)]
        return jnp.concatenate(rows + [jnp.zeros((5, 128), F32)], axis=0)

    def spread(name, first, value, peers, src):
        peer, count = peers
        tot_s[src] = value
        send_all(
            name, peer, count, lambda d: tot_s.at[src], lambda d: tot_r.at[slot(first + d - 1, 8)]
        )
        pending.append((name, tot_r.at[pl.ds(first * 8, (count - 1) * 8)]))

    def collect(name, first, value, count):
        arrived(name, tot_r.at[pl.ds(first * 8, count * 8)])
        for i in range(count):
            value = value + tot_r[(first + i) * 8 : (first + i + 1) * 8]
        return value

    col_peers = (col_peer, NC)
    yx_peers = (lambda d: row_peer(2 * d), NR // 2)
    side_peers = (side_peer, 2 * NC)

    def next_step(step, totals, iteration):
        lanes_summed = jnp.sum(totals, axis=1, keepdims=True)
        primal, dual, cross = lanes_summed[0:1], lanes_summed[1:2], lanes_summed[2:3]
        weighted = weight * primal + dual / weight + 1e-6
        shrink = 1.0 - (iteration + 2.0) ** (-0.3)
        growth = 1.0 + (iteration + 2.0) ** (-0.6)
        return (
            shrink
            * weighted
            / jnp.maximum(2.0 * jnp.abs(cross), shrink * weighted / (growth * step))
        )

    transpose_product(0)
    arrived("x0", x0g.at[pl.ds(1, NR - 1)])
    start = x0g[...]
    vector = start[:, :OWN].reshape(XR, 128)
    table = dot(own_pick_b, side_by_side(vector))
    share_table(
        0,
        jnp.concatenate([table[:, :128] + table[:, 128:], jnp.sum(start[:, OWN:], axis=0)], 0),
    )
    def turn_tile(t, carry):
        rows = pl.ds(pl.multiple_of(t * T, T), T)
        hi_t[rows] = jnp.transpose(hi[rows])
        lo_t[rows] = jnp.transpose(lo[rows])
        return carry

    lax.fori_loop(0, GROUPS * 8, turn_tile, 0)

    def next_links(now, step, pulled):
        return jnp.clip(now + (step / weight) * pulled, 0.0, ub_link)

    def patched(x, links):
        return jnp.where(link_row, placed(here, links), x)

    x_now = x0g[0, :OWN]
    y_now = yg[0, :OWN]
    x_next = next_primal(x_now, step, pull(0))
    gather_x(1, x_next)
    table = shared_table(0)
    x_link, ub_link = table[:OWN], table[OWN:]
    share_links(0)
    forward_product(0, vector, *from_links(x_link))
    x_link = next_links(x_link, step, shared_table(1))
    beside = from_links(x_link)
    x_next = patched(x_next, x_link)
    forward_product(1, gathered_x(1), *beside)
    image_old = image(0)
    image_new = image(1)
    y_next = next_dual(y_now, step, image_old, image_new)
    gather_y(1, y_next)
    value = sums(x_next - x_now, y_next - y_now, image_new - image_old)
    spread("sum_col", 0, value, col_peers, 0)
    x_now, y_now, image_old = x_next, y_next, image_new

    def at_start():
        spread("sum_row", 7, collect("sum_col", 0, value, 7), (row_peer, NR), 1)

    transpose_product(1, at_start)
    step = next_step(step, collect("sum_row", 7, tot_s[1], 31), 0)
    x_next = next_primal(x_now, step, pull(1))
    gather_x(2, x_next)
    x_link = next_links(x_link, step, link_pull(1))
    beside = from_links(x_link)
    x_next = patched(x_next, x_link)
    results[0] = x_next
    out_x = pltpu.make_async_copy(results.at[0], x_out, small_sem.at[13])
    out_x.start()
    forward_product(2, gathered_x(2), *beside)
    image_new = image(2)
    y_next = next_dual(y_now, step, image_old, image_new)
    results[1] = y_next
    out_y = pltpu.make_async_copy(results.at[1], y_out, small_sem.at[14])
    out_y.start()
    value = sums(x_next - x_now, y_next - y_now, image_new - image_old)
    spread("last_z", 38, value, side_peers, 2)
    value = collect("last_z", 38, value, 15)
    spread("last_yx", 53, value, yx_peers, 3)
    value = collect("last_yx", 53, value, 15)
    s_out[...] = next_step(step, value, 1)

    out_x.wait()
    out_y.wait()
    for name, ref in pending:
        total(name, ref).wait_send()


def on_device(
    matrix_tiles,
    tile_rows,
    tile_cols,
    tile_count,
    link_tiles,
    link_rows,
    link_target,
    link_columns,
    objective,
    upper_bound,
    right_side,
    primal_start,
    dual_start,
    primal_weight,
    step_start,
):
    flat = lambda v: v.reshape(OWN, 128)
    vmem = pl.BlockSpec(memory_space=pltpu.VMEM)
    hbm = pl.BlockSpec(memory_space=pltpu.HBM)
    n = len(PHASES)
    x, y, s = pl.pallas_call(
        kernel,
        out_shape=(
            jax.ShapeDtypeStruct((OWN, 128), F32),
            jax.ShapeDtypeStruct((OWN, 128), F32),
            jax.ShapeDtypeStruct((1, 1), F32),
        ),
        in_specs=[hbm] * 15,
        out_specs=(hbm, hbm, vmem),
        scratch_shapes=[
            pltpu.VMEM((GROUPS * 8 * T, T), F32),
            [pltpu.VMEM((1, m), jnp.int32) for m in (SLOTS, SLOTS, 1, LS, LS, LS)]
            + [pltpu.VMEM((1, 1), F32)] * 2,
            pltpu.VMEM((3, OWN, 128), F32),
            pltpu.VMEM((GROUPS * 8 * T, T), BF16),
            pltpu.VMEM((GROUPS * 8 * T, T), BF16),
            pltpu.VMEM((GROUPS * 8 * T, T), BF16),
            pltpu.VMEM((GROUPS * 8 * T, T), BF16),
            pltpu.VMEM((NR, 2 * OWN, 128), F32),
            pltpu.VMEM((3, XR, 128), F32),
            pltpu.VMEM((2, YR, 128), F32),
            pltpu.VMEM((2, XR, 128), F32),
            pltpu.VMEM((2, XR, 128), F32),
            pltpu.VMEM((3, YR, 128), F32),
            pltpu.VMEM((3, YR, 128), F32),
            [pltpu.VMEM((m * OWN, 128), F32) for m in (2, 1, 1)],
            [pltpu.VMEM((NC, m * OWN, 128), F32) for m in (2, 1, 1)],
            pltpu.VMEM((2, OWN, 128), F32),
            pltpu.VMEM((2, XR, 128), F32),
            pltpu.VMEM((4, 8, 128), F32),
            pltpu.VMEM((68 * 8, 128), F32),
            pltpu.VMEM((YR, 128), BF16),
            pltpu.VMEM((XR, 128), BF16),
            pltpu.VMEM((80, YR), BF16),
            pltpu.VMEM((80, XR), BF16),
            pltpu.VMEM((80, 16), BF16),
            pltpu.VMEM((YR, 32), BF16),
            pltpu.VMEM((16, 32), BF16),
            pltpu.VMEM((16, 128), BF16),
            pltpu.VMEM((GROUPS - 1, 16, T), F32),
            pltpu.VMEM((GROUPS - 1, 8, T), F32),
            pltpu.VMEM((2, OWN, 128), F32),
            pltpu.SemaphoreType.DMA((CHUNKS,)),
            pltpu.SemaphoreType.DMA((15,)),
            pltpu.SemaphoreType.DMA((n,)),
            pltpu.SemaphoreType.DMA((n,)),
        ],
        compiler_params=pltpu.CompilerParams(
            collective_id=0, has_side_effects=True, vmem_limit_bytes=63 * 1024 * 1024
        ),
        name="pdhg",
    )(
        matrix_tiles.reshape(SLOTS * T, T),
        link_tiles.reshape(LS * T, T),
        tile_rows.reshape(1, SLOTS),
        tile_cols.reshape(1, SLOTS),
        tile_count.reshape(1, 1),
        link_rows.reshape(1, LS),
        link_target.reshape(1, LS),
        link_columns.reshape(1, LS),
        flat(objective),
        flat(upper_bound),
        flat(right_side),
        flat(primal_start),
        flat(dual_start),
        primal_weight.reshape(1, 1),
        step_start.reshape(1, 1),
    )
    return x.reshape(-1), y.reshape(-1), s.reshape(1)


def solution(mesh):
    tile = P("row", "col", None, None, None)
    index = P("row", "col", None)
    primal = P(("col", "row"))
    dual = P(("row", "col"))
    return jax.shard_map(
        on_device,
        mesh=mesh,
        in_specs=(
            tile,
            index,
            index,
            P("row", "col"),
            tile,
            index,
            index,
            P(),
            primal,
            primal,
            dual,
            primal,
            dual,
            P(),
            P(),
        ),
        out_specs=(primal, dual, P()),
        check_vma=False,
    )
```
